128 devices in a mesh: corpus: 32 (over z, x, core), query: 4 (over y).
Axes of the slice: x: 4, y: 4, z: 4, core: 2. Of those that a mesh axis runs over, the one named last changes fastest.
Arguments:
- queries: bfloat16 [16384, 4096], P(('corpus', 'query')), may hold values from -6 to 6
- corpus: bfloat16 [65536, 4096], P(('corpus', 'query')), may hold values from -6 to 6
- shortlist: int32 [1024, 8], P(('corpus', 'query')), may hold values from 0 to 511, as said below
Outputs:
- coarse: float32 [512, 16384], P(('corpus', 'query'))
- rescored: bfloat16 [16384, 1024], P(('corpus', 'query'))
The draws below stay inside these ranges and needn't reach their ends.
Inputs may be any that keep to these rules, and one draw needn't show every extreme that they name: `shortlist`: the 8 blocks of one group differ. Block b lies with the rows of device b // 4; the 8 groups of one device name at most 1 block of any one device, and in every draw one device has exactly 1 of its blocks named by the groups of every device.
All inputs are finite; a program needn't handle non-finite values.
Results may differ from the reference program's by a relative error of at most 0.001.
Values may be sent and summed in bfloat16 or wider, within the bound.
No kernel may reach another device: no remote copies, remote signals or barrier semaphores. Data moves between devices by JAX's collectives and lax.ppermute only.
A program may use at most 128 MiB of HBM per device.

```python
import jax
import jax.numpy as jnp
from jax import lax

D = 4096
PREFIX = 256
BLOCK = 128
GROUP = 16
SHORT = 8
MOST = 1
BLK_DEV = 4
G_DEV = 8
BLOCKS = 512
PASSAGES = 65536
GROUPS = 1024
QUERIES = 16384


def draw_shortlist(key, part):
    key = jax.random.fold_in(key, 11)
    devices_all = GROUPS // G_DEV
    asked = G_DEV * SHORT
    width = devices_all * MOST
    keys = jax.random.split(key, 5)
    popular = jax.random.randint(keys[0], (devices_all,), 0, 4)
    hottest = jax.random.randint(keys[1], (), 0, devices_all)
    slot_owner = jnp.arange(width, dtype=jnp.int32) // MOST
    slot_copy = jnp.arange(width, dtype=jnp.int32) % MOST
    noise = jax.random.randint(keys[2], (devices_all, width), 0, 3072)
    score = popular[slot_owner][None, :] * 1024 + noise
    score = jnp.where(slot_owner[None, :] == hottest, 65536, score)
    score = score * width + jnp.arange(width, dtype=jnp.int32)[None, :]
    ranked = jnp.argsort(-score, axis=1, stable=True)[:, :asked].astype(jnp.int32)
    mixing = jax.random.randint(keys[3], (devices_all, asked), 0, 1 << 16) * asked + jnp.arange(asked, dtype=jnp.int32)[None, :]
    shuffle = jnp.argsort(mixing, axis=1, stable=True).astype(jnp.int32)
    chosen = jnp.take_along_axis(ranked, shuffle, axis=1)
    owner = slot_owner[chosen]
    copy_index = slot_copy[chosen]
    offsets = jax.random.randint(keys[4], (devices_all, devices_all), 0, BLK_DEV)
    local = (jnp.take_along_axis(offsets, owner, axis=1) + copy_index) % BLK_DEV
    picked = owner * BLK_DEV + local
    return picked.reshape(GROUPS, SHORT).astype(jnp.int32)


def block_levels(own_key, shape, cuts, smallest, high):
    gain = 1.0
    for position, parts in cuts:
        steps = jax.random.uniform(jax.random.fold_in(jax.random.fold_in(own_key, 6), position), (parts,), jnp.float32, smallest / len(cuts), high / len(cuts))
        gain = gain * jnp.repeat(jnp.exp(steps), shape[position] // parts).reshape((-1,) + (1,) * (len(shape) - 1 - position))
    return gain


def normal_values(key, shape, spread, bound, shards=(), held_as=jnp.bfloat16):
    result = spread * jax.random.normal(key, shape, jnp.float32)
    if shards:
        result = result * block_levels(key, shape, shards, -0.22, 0.18)
    return jnp.clip(result, -bound, bound).astype(held_as)


def setup_inputs(seed: int = 0) -> dict:
    key_of = jax.random.split(jax.random.key(seed), 4)
    return {
        "queries": normal_values(key_of[0], (QUERIES, D), 1.0, 6.0, ((0, 128),)),
        "corpus": normal_values(key_of[1], (PASSAGES, D), 1.0, 6.0, ((0, 128),)),
        "shortlist": draw_shortlist(jax.random.fold_in(key_of[3], 71), 0),
    }


def reference(queries, corpus, shortlist):
    blocks = corpus.reshape(BLOCKS, BLOCK, D)
    heads = queries[:, :PREFIX]

    def coarse_block(rows):
        scores = jnp.dot(heads, rows[:, :PREFIX].T, preferred_element_type=jnp.float32) * (PREFIX ** -0.5)
        return jnp.max(scores, axis=1)

    coarse = lax.map(coarse_block, blocks)
    groups = queries.reshape(GROUPS, GROUP, D)

    def rescore_group(item):
        members, picked = item
        rows = blocks[picked.astype(jnp.int32)].reshape(SHORT * BLOCK, D)
        scores = jnp.dot(members, rows.T, preferred_element_type=jnp.float32) * (D ** -0.5)
        return scores.astype(jnp.bfloat16)

    rescored = lax.map(rescore_group, (groups, shortlist)).reshape(QUERIES, SHORT * BLOCK)
    return coarse, rescored
```

```python
import functools

import jax
import jax.numpy as jnp
from jax import lax
from jax.experimental import pallas as pl
from jax.experimental.pallas import tpu as pltpu
from jax.sharding import PartitionSpec as P

D = 4096
PREFIX = 256
BLOCK = 128
GROUP = 16
SHORT = 8
BATCH = 8


def rescore_kernel(chunks, n_src, n_rel, scale, tab, q_ref, *refs):
    n_blocks = len(chunks) * n_rel
    blocks = refs[:n_blocks]
    prev, out, qbuf, slots, first, sems = refs[n_blocks:]
    blk_dev = 4

    if prev is not None:
        out[...] = prev[...]

    def row_copy(slot, src_row, pos):
        return pltpu.make_async_copy(
            q_ref.at[pl.ds(pl.multiple_of(src_row, GROUP), GROUP)],
            qbuf.at[pl.ds(pl.multiple_of(pos * GROUP, GROUP), GROUP)],
            sems.at[pos],
        )

    count = jnp.int32(0)
    for c, local in enumerate(chunks):
        for r in range(n_rel):
            first[c * n_rel + r] = count

            def scan(i, n):
                slot = i * n_rel + r
                v = tab[slot] - 1
                hit = (v >= 0) & (v % blk_dev == local)

                @pl.when(hit)
                def _():
                    slots[n] = slot
                    row_copy(slot, i * (8 * GROUP) + (v // blk_dev) * GROUP, n).start()

                return n + hit.astype(jnp.int32)

            count = lax.fori_loop(0, n_src, scan, count)
    first[n_blocks] = count

    def wait(n, _):
        row_copy(0, 0, n).wait()
        return 0

    lax.fori_loop(0, count, wait, 0)

    for b in range(n_blocks):
        start, end = first[b], first[b + 1]

        def step(t, _, start=start, end=end, block=blocks[b]):
            at = start + t * BATCH
            rows = qbuf[pl.ds(pl.multiple_of(at * GROUP, GROUP), BATCH * GROUP), :]
            s = lax.dot_general(
                rows, block[...], (((1,), (1,)), ((), ())), preferred_element_type=jnp.float32
            )
            s = (s * scale).astype(out.dtype)
            for m in range(BATCH):

                @pl.when(at + m < end)
                def _():
                    out[slots[at + m]] = s[m * GROUP : (m + 1) * GROUP]

            return 0

        lax.fori_loop(0, (end - start + BATCH - 1) // BATCH, step, 0)


def rescore(chunks, tab, q, blocks, prev, scale):
    n_slots = tab.shape[0]
    n_src = q.shape[0] // BLOCK
    n_rel = n_slots // n_src
    body = functools.partial(rescore_kernel, chunks, n_src, n_rel, scale)
    if prev is None:
        kernel = lambda tab, q, *refs: body(tab, q, *refs[: len(blocks)], None, *refs[len(blocks) :])
    else:
        kernel = body
    vmem = pl.BlockSpec(memory_space=pltpu.VMEM)
    extra = [] if prev is None else [prev]
    return pl.pallas_call(
        kernel,
        out_shape=jax.ShapeDtypeStruct((n_slots, GROUP, BLOCK), jnp.bfloat16),
        in_specs=[pl.BlockSpec(memory_space=pltpu.SMEM), pl.BlockSpec(memory_space=pl.ANY)]
        + [vmem] * (len(blocks) + len(extra)),
        out_specs=vmem,
        scratch_shapes=[
            pltpu.VMEM(((n_slots + BATCH) * GROUP, D), jnp.bfloat16),
            pltpu.SMEM((n_slots,), jnp.int32),
            pltpu.SMEM((len(blocks) + 1,), jnp.int32),
            pltpu.SemaphoreType.DMA((n_slots,)),
        ],
        compiler_params=pltpu.CompilerParams(vmem_limit_bytes=40 * 2**20),
        cost_estimate=pl.CostEstimate(
            flops=2 * 16 * len(chunks) * GROUP * BLOCK * D, bytes_accessed=16 * len(chunks) * GROUP * D * 2, transcendentals=0
        ),
    )(tab, q, *blocks, *extra)


def body(queries, corpus, shortlist):
    head_scale = PREFIX ** (-0.5)
    full_scale = D ** (-0.5)
    n_corpus = lax.axis_size("corpus")
    n_query = lax.axis_size("query")
    blk_dev = corpus.shape[0] // BLOCK
    j = lax.axis_index("query")

    def along(a, d):
        return lax.ppermute(a, "query", [(t, (t + d) % n_query) for t in range(n_query)])

    wanted = shortlist.reshape(-1)
    holder = wanted // blk_dev
    slot = (holder // n_query) * n_query + (holder - j) % n_query
    value = (jnp.arange(wanted.shape[0], dtype=jnp.int32) // SHORT) * blk_dev + wanted % blk_dev + 1
    ids = jnp.arange(n_corpus * n_query, dtype=jnp.int32)
    tags = jnp.max(jnp.where(slot[None, :] == ids[:, None], value[None, :], 0), axis=1)
    tab = lax.all_to_all(
        tags.reshape(n_corpus, n_query), "corpus", split_axis=0, concat_axis=0, tiled=True
    ).reshape(-1)

    q = lax.all_gather(queries, "corpus", axis=0, tiled=True)

    pieces = []
    for l in range(blk_dev):
        own = corpus[l * BLOCK : (l + 1) * BLOCK]
        before = along(own, 1)
        after = along(own, -1)
        across = along(before, 1) if l % 2 == 0 else along(after, -1)
        pieces.append([own, after, across, before])

    heads = q[:, :PREFIX]
    best = []
    for l in range(blk_dev):
        ch = jnp.concatenate([p[:, :PREFIX] for p in pieces[l]], axis=0)
        s = jnp.einsum("qd,pd->qp", heads, ch, preferred_element_type=jnp.float32) * head_scale
        best.append(jnp.max(s.reshape(heads.shape[0], n_query, BLOCK), axis=2).T)
    best = jnp.stack(best, axis=1)
    back = jnp.stack([best[0], along(best[1], 1), along(best[2], 2), along(best[3], -1)])
    back = back.reshape(n_query, blk_dev, n_corpus, BLOCK)
    coarse = jnp.stack(
        [lax.dynamic_index_in_dim(back, (j - t) % n_query, 0, keepdims=False) for t in range(n_query)], axis=2
    ).reshape(blk_dev, -1)

    flat = [b for l in range(blk_dev - 1) for b in pieces[l]]
    answers = rescore(tuple(range(blk_dev - 1)), tab, q, flat, None, full_scale)
    answers = rescore((blk_dev - 1,), tab, q, pieces[blk_dev - 1], answers, full_scale)
    returned = lax.all_to_all(
        answers.reshape(n_corpus, n_query, GROUP, BLOCK), "corpus", split_axis=0, concat_axis=0, tiled=True
    )
    returned = returned.reshape(n_corpus * n_query, GROUP, BLOCK)[slot]
    rescored = returned.reshape(-1, SHORT, GROUP, BLOCK).transpose(0, 2, 1, 3).reshape(-1, SHORT * BLOCK)
    return (coarse, rescored)


def solution(mesh):
    spec = P(("corpus", "query"), None)
    return jax.shard_map(
        body, mesh=mesh, in_specs=(spec, spec, spec), out_specs=(spec, spec), check_vma=False
    )
```

```python
import functools

import jax
import jax.numpy as jnp
from jax import lax
from jax.experimental import pallas as pl
from jax.experimental.pallas import tpu as pltpu
from jax.sharding import PartitionSpec as P

D = 4096
PREFIX = 256
BLOCK = 128
GROUP = 16
SHORT = 8
BATCH = 8
TILE = 256

SMEM = pl.BlockSpec(memory_space=pltpu.SMEM)
VMEM = pl.BlockSpec(memory_space=pltpu.VMEM)


def list_kernel(order, blk_dev, n_src, n_rel, tab, rows, slots, first):
    def clear(n, _):
        rows[n] = 0
        slots[n] = 0
        return 0

    lax.fori_loop(0, n_src * n_rel, clear, 0)
    count = jnp.int32(0)
    for b, (local, r) in enumerate(order):
        first[b] = count

        def scan(i, n, local=local, r=r):
            slot = i * n_rel + r
            v = tab[slot] - 1
            hit = (v >= 0) & (v % blk_dev == local)

            @pl.when(hit)
            def _():
                slots[n] = slot
                rows[n] = i * BLOCK + (v // blk_dev) * GROUP

            return n + hit.astype(jnp.int32)

        count = lax.fori_loop(0, n_src, scan, count)
    first[len(order)] = count


def score_kernel(b0, groups, n_prev, full_scale, head_scale, rows, slots, first, q_ref, *refs):
    n_blocks = sum(n for _, n in groups)
    blocks = refs[:n_blocks]
    prev = refs[n_blocks : n_blocks + n_prev]
    out = refs[n_blocks + n_prev]
    best = refs[n_blocks + n_prev + 1 : n_blocks + n_prev + 1 + len(groups)]
    qbuf, hbuf, cbuf, sems, hsem = refs[n_blocks + n_prev + 1 + len(groups) :]

    def row_copy(src_row, pos):
        return pltpu.make_async_copy(
            q_ref.at[pl.ds(pl.multiple_of(src_row, GROUP), GROUP)],
            qbuf.at[pl.ds(pl.multiple_of(pos * GROUP, GROUP), GROUP)],
            sems.at[pos],
        )

    heads = pltpu.make_async_copy(q_ref.at[:, pl.ds(0, PREFIX)], hbuf, hsem)
    heads.start()
    base = first[b0]
    total = first[b0 + n_blocks] - base

    def start(n, _):
        row_copy(rows[base + n], n).start()
        return 0

    lax.fori_loop(0, total, start, 0)

    for b in range(n_blocks):
        cbuf[b * BLOCK : (b + 1) * BLOCK] = blocks[b][:, :PREFIX]
    if n_prev:
        out[...] = prev[0][...]
        for ref, old in zip(best, prev[1:]):
            ref[...] = old[...]
    heads.wait()

    def coarse(t, _):
        h = hbuf[pl.ds(pl.multiple_of(t * TILE, TILE), TILE), :]
        at = 0
        for ref, (l0, n) in zip(best, groups):
            s = lax.dot_general(
                cbuf[at * BLOCK : (at + n) * BLOCK], h, (((1,), (1,)), ((), ())), preferred_element_type=jnp.float32
            )
            top = jnp.max(s.reshape(n, BLOCK, TILE), axis=1) * head_scale
            ref[l0 : l0 + n, pl.ds(pl.multiple_of(t * TILE, TILE), TILE)] = top
            at += n
        return 0

    lax.fori_loop(0, hbuf.shape[0] // TILE, coarse, 0)

    waited = jnp.int32(0)
    for b in range(n_blocks):
        lo, hi = first[b0 + b] - base, first[b0 + b + 1] - base

        def step(t, waited, lo=lo, hi=hi, block=blocks[b]):
            at = lo + t * BATCH
            upto = jnp.minimum(at + BATCH, total)

            def wait(n, _):
                row_copy(0, n).wait()
                return 0

            lax.fori_loop(waited, upto, wait, 0)
            part = qbuf[pl.ds(pl.multiple_of(at * GROUP, GROUP), BATCH * GROUP), :]
            s = lax.dot_general(part, block[...], (((1,), (1,)), ((), ())), preferred_element_type=jnp.float32)
            s = (s * full_scale).astype(out.dtype)
            for m in range(BATCH):

                @pl.when(at + m < hi)
                def _():
                    out[slots[base + at + m]] = s[m * GROUP : (m + 1) * GROUP]

            return jnp.maximum(waited, upto)

        waited = lax.fori_loop(0, (hi - lo + BATCH - 1) // BATCH, step, waited)


def score(b0, groups, lists, q, blocks, prev, blk_dev, n_slots):
    n_q = q.shape[0]
    n_blocks = len(blocks)
    kernel = functools.partial(score_kernel, b0, groups, len(prev), D ** (-0.5), PREFIX ** (-0.5))
    return pl.pallas_call(
        kernel,
        out_shape=[jax.ShapeDtypeStruct((n_slots, GROUP, BLOCK), jnp.bfloat16)]
        + [jax.ShapeDtypeStruct((blk_dev, n_q), jnp.float32)] * len(groups),
        in_specs=[SMEM] * 3 + [pl.BlockSpec(memory_space=pl.ANY)] + [VMEM] * (n_blocks + len(prev)),
        out_specs=[VMEM] * (1 + len(groups)),
        scratch_shapes=[
            pltpu.VMEM(((n_slots + BATCH) * GROUP, D), jnp.bfloat16),
            pltpu.VMEM((n_q, PREFIX), jnp.bfloat16),
            pltpu.VMEM((n_blocks * BLOCK, PREFIX), jnp.bfloat16),
            pltpu.SemaphoreType.DMA((n_slots,)),
            pltpu.SemaphoreType.DMA(()),
        ],
        compiler_params=pltpu.CompilerParams(vmem_limit_bytes=48 * 2**20),
        cost_estimate=pl.CostEstimate(
            flops=2 * n_blocks * BLOCK * (n_q * PREFIX + 4 * GROUP * D), bytes_accessed=n_blocks * 2**20, transcendentals=0
        ),
    )(*lists, q, *blocks, *prev)


def body(queries, corpus, shortlist):
    n_corpus = lax.axis_size("corpus")
    n_query = lax.axis_size("query")
    n_slots = n_corpus * n_query
    blk_dev = corpus.shape[0] // BLOCK
    j = lax.axis_index("query")

    def along(a, d):
        return lax.ppermute(a, "query", [(t, (t + d) % n_query) for t in range(n_query)])

    q = lax.all_gather(queries, "corpus", axis=0, tiled=True)

    pieces = []
    for l in range(blk_dev):
        own = corpus[l * BLOCK : (l + 1) * BLOCK]
        before = along(own, 1)
        after = along(own, -1)
        across = along(before, 1) if l % 2 == 0 else along(after, -1)
        pieces.append([own, after, across, before])

    wanted, _ = lax.optimization_barrier((shortlist.reshape(-1), pieces[0][3]))
    holder = wanted // blk_dev
    slot = (holder // n_query) * n_query + (holder - j) % n_query
    value = (jnp.arange(wanted.shape[0], dtype=jnp.int32) // SHORT) * blk_dev + wanted % blk_dev + 1
    ids = jnp.arange(n_slots, dtype=jnp.int32)
    tags = jnp.max(jnp.where(slot[None, :] == ids[:, None], value[None, :], 0), axis=1)
    tab = lax.all_to_all(
        tags.reshape(n_corpus, n_query), "corpus", split_axis=0, concat_axis=0, tiled=True
    ).reshape(-1)

    order = [(l, r) for r in (0, 1, 3, 2) for l in range(blk_dev)]
    lists = pl.pallas_call(
        functools.partial(list_kernel, order, blk_dev, n_corpus, n_query),
        out_shape=[jax.ShapeDtypeStruct((n,), jnp.int32) for n in (n_slots, n_slots, len(order) + 1)],
        in_specs=[SMEM],
        out_specs=[SMEM] * 3,
    )(tab)

    early = [pieces[l][r] for l, r in order[:-1]]
    late = [pieces[l][r] for l, r in order[-1:]]
    answers, c0, c1, c3, c2 = score(
        0, [(0, blk_dev)] * 3 + [(0, blk_dev - 1)], lists, q, early, [], blk_dev, n_slots
    )
    answers, c2 = score(len(order) - 1, [(blk_dev - 1, 1)], lists, q, late, [answers, c2], blk_dev, n_slots)

    back = jnp.stack([c0, along(c1, 1), along(c2, 2), along(c3, -1)])
    back = back.reshape(n_query, blk_dev, n_corpus, BLOCK)
    coarse = jnp.stack(
        [lax.dynamic_index_in_dim(back, (j - t) % n_query, 0, keepdims=False) for t in range(n_query)], axis=2
    ).reshape(blk_dev, -1)

    returned = lax.all_to_all(
        answers.reshape(n_corpus, n_query, GROUP, BLOCK), "corpus", split_axis=0, concat_axis=0, tiled=True
    )
    returned = returned.reshape(n_slots, GROUP, BLOCK)[slot]
    rescored = returned.reshape(-1, SHORT, GROUP, BLOCK).transpose(0, 2, 1, 3).reshape(-1, SHORT * BLOCK)
    return (coarse, rescored)


def solution(mesh):
    spec = P(("corpus", "query"), None)
    return jax.shard_map(
        body, mesh=mesh, in_specs=(spec, spec, spec), out_specs=(spec, spec), check_vma=False
    )
```

```python
import functools

import jax
import jax.numpy as jnp
from jax import lax
from jax.experimental import pallas as pl
from jax.experimental.pallas import tpu as pltpu
from jax.sharding import PartitionSpec as P

D = 4096
PREFIX = 256
BLOCK = 128
GROUP = 16
SHORT = 8
BATCH = 8
TILE = 256

SMEM = pl.BlockSpec(memory_space=pltpu.SMEM)
VMEM = pl.BlockSpec(memory_space=pltpu.VMEM)


def list_kernel(order, blk_dev, n_src, n_rel, tab, rows, slots, first):
    def clear(n, _):
        rows[n] = 0
        slots[n] = 0
        return 0

    lax.fori_loop(0, n_src * n_rel, clear, 0)
    count = jnp.int32(0)
    for b, (local, r) in enumerate(order):
        first[b] = count

        def scan(i, n, local=local, r=r):
            slot = i * n_rel + r
            v = tab[slot] - 1
            hit = (v >= 0) & (v % blk_dev == local)

            @pl.when(hit)
            def _():
                slots[n] = slot
                rows[n] = i * BLOCK + (v // blk_dev) * GROUP

            return n + hit.astype(jnp.int32)

        count = lax.fori_loop(0, n_src, scan, count)
    first[len(order)] = count


def score_kernel(b0, groups, n_prev, full_scale, head_scale, rows, slots, first, q_ref, *refs):
    n_blocks = sum(len(g) for g in groups)
    refs = list(refs)
    take = lambda n: [refs.pop(0) for _ in range(n)]
    blocks, prev = take(n_blocks), take(n_prev)
    (out,), best = take(1), take(len(groups))
    heads = prev.pop(0) if n_prev else refs.pop(0)
    qbuf, cbuf, sems, hsems = refs
    n_tiles = heads.shape[0] // TILE

    def row_copy(src_row, pos):
        return pltpu.make_async_copy(
            q_ref.at[pl.ds(pl.multiple_of(src_row, GROUP), GROUP)],
            qbuf.at[pl.ds(pl.multiple_of(pos * GROUP, GROUP), GROUP)],
            sems.at[pos],
        )

    def head_copy(t):
        span = pl.ds(pl.multiple_of(t * TILE, TILE), TILE)
        return pltpu.make_async_copy(q_ref.at[span, pl.ds(0, PREFIX)], heads.at[span], hsems.at[t])

    if not n_prev:
        for t in range(n_tiles):
            head_copy(t).start()
    base = first[b0]
    total = first[b0 + n_blocks] - base

    def start(n, _):
        row_copy(rows[base + n], n).start()
        return 0

    lax.fori_loop(0, total, start, 0)

    for b in range(n_blocks):
        cbuf[b * BLOCK : (b + 1) * BLOCK] = blocks[b][:, :PREFIX]
    if n_prev:
        for ref, old in zip([out] + best, prev):
            ref[...] = old[...]

    def coarse(t, _):
        span = pl.ds(pl.multiple_of(t * TILE, TILE), TILE)
        if not n_prev:
            head_copy(t).wait()
        h = heads[span, :]
        at = 0
        for ref, locals_ in zip(best, groups):
            n = len(locals_)
            s = lax.dot_general(
                cbuf[at * BLOCK : (at + n) * BLOCK], h, (((1,), (1,)), ((), ())), preferred_element_type=jnp.float32
            )
            top = jnp.max(s.reshape(n, BLOCK, TILE), axis=1) * head_scale
            for m, l in enumerate(locals_):
                ref[l : l + 1, span] = top[m : m + 1]
            at += n
        return 0

    lax.fori_loop(0, n_tiles, coarse, 0)

    waited = jnp.int32(0)
    for b in range(n_blocks):
        lo, hi = first[b0 + b] - base, first[b0 + b + 1] - base

        def step(t, waited, lo=lo, hi=hi, block=blocks[b]):
            at = lo + t * BATCH
            upto = jnp.minimum(at + BATCH, total)

            def wait(n, _):
                row_copy(0, n).wait()
                return 0

            lax.fori_loop(waited, upto, wait, 0)
            part = qbuf[pl.ds(pl.multiple_of(at * GROUP, GROUP), BATCH * GROUP), :]
            s = lax.dot_general(part, block[...], (((1,), (1,)), ((), ())), preferred_element_type=jnp.float32)
            s = (s * full_scale).astype(out.dtype)
            for m in range(BATCH):

                @pl.when(at + m < hi)
                def _():
                    out[slots[base + at + m]] = s[m * GROUP : (m + 1) * GROUP]

            return jnp.maximum(waited, upto)

        waited = lax.fori_loop(0, (hi - lo + BATCH - 1) // BATCH, step, waited)


def score(b0, groups, lists, q, blocks, prev, blk_dev, n_slots):
    n_q = q.shape[0]
    n_blocks = len(blocks)
    kernel = functools.partial(score_kernel, b0, groups, len(prev), D ** (-0.5), PREFIX ** (-0.5))
    out_shape = [jax.ShapeDtypeStruct((n_slots, GROUP, BLOCK), jnp.bfloat16)]
    out_shape += [jax.ShapeDtypeStruct((blk_dev, n_q), jnp.float32)] * len(groups)
    if not prev:
        out_shape.append(jax.ShapeDtypeStruct((n_q, PREFIX), jnp.bfloat16))
    return pl.pallas_call(
        kernel,
        out_shape=out_shape,
        in_specs=[SMEM] * 3 + [pl.BlockSpec(memory_space=pl.ANY)] + [VMEM] * (n_blocks + len(prev)),
        out_specs=[VMEM] * len(out_shape),
        scratch_shapes=[
            pltpu.VMEM(((n_slots + BATCH) * GROUP, D), jnp.bfloat16),
            pltpu.VMEM((n_blocks * BLOCK, PREFIX), jnp.bfloat16),
            pltpu.SemaphoreType.DMA((n_slots,)),
            pltpu.SemaphoreType.DMA((n_q // TILE,)),
        ],
        compiler_params=pltpu.CompilerParams(vmem_limit_bytes=40 * 2**20),
        cost_estimate=pl.CostEstimate(
            flops=2 * n_blocks * BLOCK * (n_q * PREFIX + 4 * GROUP * D), bytes_accessed=n_blocks * 2**20, transcendentals=0
        ),
    )(*lists, q, *blocks, *prev)


def body(queries, corpus, shortlist):
    n_corpus = lax.axis_size("corpus")
    n_query = lax.axis_size("query")
    n_slots = n_corpus * n_query
    blk_dev = corpus.shape[0] // BLOCK
    j = lax.axis_index("query")

    def along(a, d):
        return lax.ppermute(a, "query", [(t, (t + d) % n_query) for t in range(n_query)])

    q = lax.all_gather(queries, "corpus", axis=0, tiled=True)

    wanted = shortlist.reshape(-1)
    holder = wanted // blk_dev
    slot = (holder // n_query) * n_query + (holder - j) % n_query
    value = (jnp.arange(wanted.shape[0], dtype=jnp.int32) // SHORT) * blk_dev + wanted % blk_dev + 1
    ids = jnp.arange(n_slots, dtype=jnp.int32)
    tags = jnp.max(jnp.where(slot[None, :] == ids[:, None], value[None, :], 0), axis=1)
    tab = lax.all_to_all(
        tags.reshape(n_corpus, n_query), "corpus", split_axis=0, concat_axis=0, tiled=True
    ).reshape(-1)

    order = [(l, 0) for l in range(4)] + [(l, 2) for l in range(4)] + [(0, 3), (3, 3), (1, 1), (2, 1)]
    order += [(0, 1), (3, 1), (1, 3), (2, 3)]
    lists = pl.pallas_call(
        functools.partial(list_kernel, order, blk_dev, n_corpus, n_query),
        out_shape=[jax.ShapeDtypeStruct((n,), jnp.int32) for n in (n_slots, n_slots, len(order) + 1)],
        in_specs=[SMEM],
        out_specs=[SMEM] * 3,
    )(tab)

    piece = {(l, 0): corpus[l * BLOCK : (l + 1) * BLOCK] for l in range(4)}
    for l, r, step in ((0, 3, 1), (3, 3, 1), (1, 1, -1), (2, 1, -1)):
        piece[l, r] = along(piece[l, 0], step)
    for l, r, step in ((0, 3, 1), (3, 3, 1), (1, 1, -1), (2, 1, -1)):
        block, _ = lax.optimization_barrier((piece[l, r], lists[0]))
        piece[l, 2] = along(block, step)
    for l, r, step, after in ((1, 3, 1, 0), (2, 3, 1, 3), (0, 1, -1, 1), (3, 1, -1, 2)):
        own, _ = lax.optimization_barrier((piece[l, 0], piece[after, 2]))
        piece[l, r] = along(own, step)

    n_early = 12
    early = [piece[lr] for lr in order[:n_early]]
    late = [piece[lr] for lr in order[n_early:]]
    answers, c0, c2, c3, c1, heads = score(
        0, [range(4), range(4), (0, 3), (1, 2)], lists, q, early, [], blk_dev, n_slots
    )
    answers, c1, c3 = score(n_early, [(0, 3), (1, 2)], lists, q, late, [heads, answers, c1, c3], blk_dev, n_slots)

    back = jnp.stack([c0, along(c1, 1), along(c2, 2), along(c3, -1)])
    back = back.reshape(n_query, blk_dev, n_corpus, BLOCK)
    coarse = jnp.stack(
        [lax.dynamic_index_in_dim(back, (j - t) % n_query, 0, keepdims=False) for t in range(n_query)], axis=2
    ).reshape(blk_dev, -1)

    returned = lax.all_to_all(
        answers.reshape(n_corpus, n_query, GROUP, BLOCK), "corpus", split_axis=0, concat_axis=0, tiled=True
    )
    returned = returned.reshape(n_slots, GROUP, BLOCK)[slot]
    rescored = returned.reshape(-1, SHORT, GROUP, BLOCK).transpose(0, 2, 1, 3).reshape(-1, SHORT * BLOCK)
    return (coarse, rescored)


def solution(mesh):
    spec = P(("corpus", "query"), None)
    return jax.shard_map(
        body, mesh=mesh, in_specs=(spec, spec, spec), out_specs=(spec, spec), check_vma=False
    )
```

```python
import functools

import jax
import jax.numpy as jnp
from jax import lax
from jax.experimental import pallas as pl
from jax.experimental.pallas import tpu as pltpu
from jax.sharding import PartitionSpec as P

D = 4096
PREFIX = 256
BLOCK = 128
GROUP = 16
SHORT = 8
BATCH = 8
TILE = 256
MIB = 2**20

SMEM = pl.BlockSpec(memory_space=pltpu.SMEM)
VMEM = pl.BlockSpec(memory_space=pltpu.VMEM)
ANY = pl.BlockSpec(memory_space=pl.ANY)


def list_kernel(steps, blk_dev, n_src, n_rel, tab, rows, slots, first):
    def clear(n, _):
        rows[n] = 0
        slots[n] = 0
        return 0

    lax.fori_loop(0, n_src * n_rel, clear, 0)
    count = jnp.int32(0)
    for b in range(len(steps) * blk_dev):
        first[b] = count

        def scan(i, n, local=b % blk_dev, r=steps[b // blk_dev]):
            v = tab[i * n_rel + r] - 1
            hit = (v >= 0) & (v % blk_dev == local)

            @pl.when(hit)
            def _():
                slots[n] = i
                rows[n] = i * BLOCK + (v // blk_dev) * GROUP

            return n + hit.astype(jnp.int32)

        count = lax.fori_loop(0, n_src, scan, count)
    first[len(steps) * blk_dev] = count


def coarse_steps(heads, arrays, cbuf, best, scale):
    at = 0
    for group in arrays:
        for ref in group:
            cbuf[at : at + ref.shape[0]] = ref[:, :PREFIX]
            at += ref.shape[0]

    def tile(t, _):
        span = pl.ds(pl.multiple_of(t * TILE, TILE), TILE)
        h = heads[span, :]
        at = 0
        for group, out in zip(arrays, best):
            n = sum(ref.shape[0] for ref in group)
            s = lax.dot_general(
                cbuf[at : at + n], h, (((1,), (1,)), ((), ())), preferred_element_type=jnp.float32
            )
            out[:, span] = jnp.max(s.reshape(n // BLOCK, BLOCK, TILE), axis=1) * scale
            at += n
        return 0

    lax.fori_loop(0, heads.shape[0] // TILE, tile, 0)


def coarse_kernel(scale, heads, *refs):
    n = (len(refs) - 1) // 2
    coarse_steps(heads, [[ref] for ref in refs[:n]], refs[2 * n], refs[n : 2 * n], scale)


def score_kernel(b0, widths, scale, head_scale, rows, slots, first, q_ref, *refs):
    n_arrays = sum(widths)
    refs = list(refs)
    arrays = [refs.pop(0) for _ in range(n_arrays)]
    if len(widths) == 1:
        heads, out, best, qbuf, cbuf, sems = refs
    else:
        out, qbuf, sems = refs
    n_rel = len(widths)

    def row_copy(src_row, pos):
        return pltpu.make_async_copy(
            q_ref.at[pl.ds(pl.multiple_of(src_row, GROUP), GROUP)],
            qbuf.at[pl.ds(pl.multiple_of(pos * GROUP, GROUP), GROUP)],
            sems.at[pos],
        )

    n_blocks = sum(ref.shape[0] // BLOCK for ref in arrays)
    base = first[b0]
    total = first[b0 + n_blocks] - base

    def start(n, _):
        row_copy(rows[base + n], n).start()
        return 0

    lax.fori_loop(0, total, start, 0)
    if n_rel == 1:
        coarse_steps(heads, [arrays], cbuf, [best], head_scale)

    waited = jnp.int32(0)
    b = b0
    for ref, rel in zip(arrays, [k for k, n in enumerate(widths) for _ in range(n)]):
        for local in range(ref.shape[0] // BLOCK):
            lo, hi = first[b] - base, first[b + 1] - base
            b += 1

            def step(t, waited, lo=lo, hi=hi, ref=ref, local=local, rel=rel):
                at = lo + t * BATCH
                upto = jnp.minimum(at + BATCH, total)

                def wait(n, _):
                    row_copy(0, n).wait()
                    return 0

                lax.fori_loop(waited, upto, wait, 0)
                part = qbuf[pl.ds(pl.multiple_of(at * GROUP, GROUP), BATCH * GROUP), :]
                block = ref[local * BLOCK : (local + 1) * BLOCK, :]
                s = lax.dot_general(part, block, (((1,), (1,)), ((), ())), preferred_element_type=jnp.float32)
                s = (s * scale).astype(out.dtype)
                for m in range(BATCH):

                    @pl.when(at + m < hi)
                    def _():
                        out[slots[base + at + m] * n_rel + rel] = s[m * GROUP : (m + 1) * GROUP]

                return jnp.maximum(waited, upto)

            waited = lax.fori_loop(0, (hi - lo + BATCH - 1) // BATCH, step, waited)


def coarse_call(heads, arrays, blk_dev):
    out = jax.ShapeDtypeStruct((blk_dev, heads.shape[0]), jnp.float32)
    passages = sum(a.shape[0] for a in arrays)
    return pl.pallas_call(
        functools.partial(coarse_kernel, PREFIX ** (-0.5)),
        out_shape=[out] * len(arrays),
        in_specs=[VMEM] * (1 + len(arrays)),
        out_specs=[VMEM] * len(arrays),
        scratch_shapes=[pltpu.VMEM((passages, PREFIX), jnp.bfloat16)],
        compiler_params=pltpu.CompilerParams(vmem_limit_bytes=24 * MIB),
        cost_estimate=pl.CostEstimate(
            flops=2 * passages * heads.shape[0] * PREFIX, bytes_accessed=8 * MIB, transcendentals=0
        ),
    )(heads, *arrays)


def score_call(b0, groups, lists, q, heads, n_src, blk_dev):
    arrays = [a for group in groups for a in group]
    n_slots = n_src * len(groups)
    passages = sum(a.shape[0] for a in arrays)
    out_shape = [jax.ShapeDtypeStruct((n_slots, GROUP, BLOCK), jnp.bfloat16)]
    scratch = [pltpu.VMEM(((n_slots + BATCH) * GROUP, D), jnp.bfloat16)]
    more = []
    if len(groups) == 1:
        more = [heads]
        out_shape.append(jax.ShapeDtypeStruct((blk_dev, q.shape[0]), jnp.float32))
        scratch.append(pltpu.VMEM((passages, PREFIX), jnp.bfloat16))
    scratch.append(pltpu.SemaphoreType.DMA((n_slots,)))
    kernel = functools.partial(
        score_kernel, b0, [len(group) for group in groups], D ** (-0.5), PREFIX ** (-0.5)
    )
    return pl.pallas_call(
        kernel,
        out_shape=out_shape,
        in_specs=[SMEM] * 3 + [ANY] + [VMEM] * (len(arrays) + len(more)),
        out_specs=[VMEM] * len(out_shape),
        scratch_shapes=scratch,
        compiler_params=pltpu.CompilerParams(vmem_limit_bytes=(32 if len(groups) > 1 else 24) * MIB),
        cost_estimate=pl.CostEstimate(flops=2 * passages * 64 * D, bytes_accessed=passages * D * 4, transcendentals=0),
    )(*lists, q, *arrays, *more)


def pick_kernel(n_rel, slot, near, far, out):
    for e in range(slot.shape[0]):
        i, r = slot[e] // n_rel, slot[e] % n_rel
        k = jnp.where(r == 3, 2, jnp.minimum(r, 1))
        g, s = e // SHORT, e % SHORT
        out[g * GROUP : (g + 1) * GROUP, s * BLOCK : (s + 1) * BLOCK] = jnp.where(
            r == 2, far[i], near[i * (n_rel - 1) + k]
        )


def body(queries, corpus, shortlist):
    n_corpus = lax.axis_size("corpus")
    n_query = lax.axis_size("query")
    n_slots = n_corpus * n_query
    blk_dev = corpus.shape[0] // BLOCK
    half = corpus.shape[0] // 2
    j = lax.axis_index("query")

    def along(a, d):
        return lax.ppermute(a, "query", [(t, (t + d) % n_query) for t in range(n_query)])

    def exchange(a):
        return lax.all_to_all(a, "corpus", split_axis=0, concat_axis=0, tiled=True)

    q = lax.all_gather(queries, "corpus", axis=0, tiled=True)

    before = along(corpus, 1)
    after = along(corpus, -1)

    wanted = shortlist.reshape(-1)
    holder = wanted // blk_dev
    slot = (holder // n_query) * n_query + (holder - j) % n_query
    value = (jnp.arange(wanted.shape[0], dtype=jnp.int32) // SHORT) * blk_dev + wanted % blk_dev + 1
    ids = jnp.arange(n_slots, dtype=jnp.int32)
    tags = jnp.max(jnp.where(slot[None, :] == ids[:, None], value[None, :], 0), axis=1)
    tab = exchange(tags.reshape(n_corpus, n_query)).reshape(-1)
    steps = (0, 1, 3, 2)
    n_lists = len(steps) * blk_dev + 1
    lists = pl.pallas_call(
        functools.partial(list_kernel, steps, blk_dev, n_corpus, n_query),
        out_shape=[jax.ShapeDtypeStruct((n,), jnp.int32) for n in (n_slots, n_slots, n_lists)],
        in_specs=[SMEM],
        out_specs=[SMEM] * 3,
    )(tab)

    heads = exchange(jnp.broadcast_to(queries[None, :, :PREFIX], (n_corpus, queries.shape[0], PREFIX)))
    heads = heads.reshape(-1, PREFIX)

    before, after, heads, *lists = lax.optimization_barrier((before, after, heads, *lists))
    low = along(before[:half], 1)
    high = along(after[half:], -1)

    c0, c1, c3 = coarse_call(heads, [corpus, after, before], blk_dev)
    (near,) = score_call(0, [[corpus], [after], [before]], lists, q, None, n_corpus, blk_dev)
    near = exchange(near.reshape(n_corpus, -1, BLOCK))
    far, c2 = score_call(3 * blk_dev, [[low, high]], lists, q, heads, n_corpus, blk_dev)
    far = exchange(far)

    back = jnp.stack([c0, along(c1, 1), along(c2, 2), along(c3, -1)])
    back = back.reshape(n_query, blk_dev, n_corpus, BLOCK)
    coarse = jnp.stack(
        [lax.dynamic_index_in_dim(back, (j - t) % n_query, 0, keepdims=False) for t in range(n_query)], axis=2
    ).reshape(blk_dev, -1)

    rescored = pl.pallas_call(
        functools.partial(pick_kernel, n_query),
        out_shape=jax.ShapeDtypeStruct((queries.shape[0], SHORT * BLOCK), jnp.bfloat16),
        in_specs=[SMEM, VMEM, VMEM],
        out_specs=VMEM,
    )(slot, near.reshape(-1, GROUP, BLOCK), far)
    return (coarse, rescored)


def solution(mesh):
    spec = P(("corpus", "query"), None)
    return jax.shard_map(
        body, mesh=mesh, in_specs=(spec, spec, spec), out_specs=(spec, spec), check_vma=False
    )
```

```python
import functools

import jax
import jax.numpy as jnp
from jax import lax
from jax.experimental import pallas as pl
from jax.experimental.pallas import tpu as pltpu
from jax.sharding import PartitionSpec as P

D = 4096
PREFIX = 256
BLOCK = 128
GROUP = 16
SHORT = 8
BATCH = 8
PAIR = 2
TILE = 512
MIB = 2**20

SMEM = pl.BlockSpec(memory_space=pltpu.SMEM)
VMEM = pl.BlockSpec(memory_space=pltpu.VMEM)
ANY = pl.BlockSpec(memory_space=pl.ANY)


def list_kernel(order, blk_dev, n_src, n_rel, tab, lists):
    most = n_src * n_rel

    def clear(n, _):
        lists[n] = 0
        return 0

    lax.fori_loop(0, 2 * most, clear, 0)
    count = jnp.int32(0)
    for b, (local, r) in enumerate(order):
        lists[2 * most + b] = count

        def scan(i, n, local=local, r=r):
            v = tab[i * n_rel + r] - 1
            hit = (v >= 0) & (v % blk_dev == local)

            @pl.when(hit)
            def _():
                lists[n] = i * BLOCK + (v // blk_dev) * GROUP
                lists[most + n] = i

            return n + hit.astype(jnp.int32)

        count = lax.fori_loop(0, n_src, scan, count)
    lists[2 * most + len(order)] = count


def score_kernel(b0, order, most, n_rel, scale, head_scale, lists, q_ref, *refs):
    n_arrays = len(order) // PAIR
    arrays, refs = refs[:n_arrays], refs[n_arrays:]
    coarse = len(refs) > 5
    if coarse:
        prev, heads, out, best, cbuf, hsems, qbuf, abuf, sems, asems = refs
    else:
        out, qbuf, abuf, sems, asems = refs
    wide = PAIR * BLOCK
    wholes = [pltpu.make_async_copy(ref, abuf.at[k], asems.at[k]) for k, ref in enumerate(arrays)]
    if coarse:
        tops = [
            pltpu.make_async_copy(ref.at[:, pl.ds(0, PREFIX)], cbuf.at[pl.ds(k * wide, wide)], hsems.at[k])
            for k, ref in enumerate(arrays)
        ]
        for copy in tops:
            copy.start()

    def row_copy(src_row, pos):
        return pltpu.make_async_copy(
            q_ref.at[pl.ds(pl.multiple_of(src_row, GROUP), GROUP)],
            qbuf.at[pl.ds(pl.multiple_of(pos * GROUP, GROUP), GROUP)],
            sems.at[pos],
        )

    first = 2 * most + b0
    base = lists[first]
    total = lists[first + len(order)] - base

    def start(n, _):
        row_copy(lists[base + n], n).start()
        return 0

    lax.fori_loop(0, total, start, 0)
    for copy in wholes:
        copy.start()
    if coarse:
        out[...] = prev[...]
        for copy in tops:
            copy.wait()

        def tile(t, _):
            span = pl.ds(pl.multiple_of(t * TILE, TILE), TILE)
            h = heads[span, :]
            for k in range(n_arrays):
                s = lax.dot_general(
                    cbuf[k * wide : (k + 1) * wide], h, (((1,), (1,)), ((), ())), preferred_element_type=jnp.float32
                )
                top = jnp.max(s.reshape(PAIR, BLOCK, TILE), axis=1) * head_scale
                best[k * PAIR : (k + 1) * PAIR, span] = top
            return 0

        lax.fori_loop(0, heads.shape[0] // TILE, tile, 0, unroll=2)

    waited = jnp.int32(0)
    for b, (_, rel) in enumerate(order):
        if b % PAIR == 0:
            wholes[b // PAIR].wait()
        lo, hi = lists[first + b] - base, lists[first + b + 1] - base

        def step(t, waited, lo=lo, hi=hi, block=abuf.at[b // PAIR, pl.ds(b % PAIR * BLOCK, BLOCK)], rel=rel):
            at = lo + t * BATCH
            upto = jnp.minimum(at + BATCH, total)

            def wait(n, _):
                row_copy(0, n).wait()
                return 0

            lax.fori_loop(waited, upto, wait, 0)
            part = qbuf[pl.ds(pl.multiple_of(at * GROUP, GROUP), BATCH * GROUP), :]
            s = lax.dot_general(part, block[...], (((1,), (1,)), ((), ())), preferred_element_type=jnp.float32)
            s = (s * scale).astype(out.dtype)
            for m in range(BATCH):

                @pl.when(at + m < hi)
                def _():
                    out[lists[most + base + at + m] * n_rel + rel] = s[m * GROUP : (m + 1) * GROUP]

            return jnp.maximum(waited, upto)

        waited = lax.fori_loop(0, (hi - lo + BATCH - 1) // BATCH, step, waited)


def score(b0, order, arrays, lists, q, more, n_src, n_rel):
    most = n_src * len({r for _, r in order})
    passages = len(order) * BLOCK
    out_shape = [jax.ShapeDtypeStruct((n_src * n_rel, GROUP, BLOCK), jnp.bfloat16)]
    scratch = [
        pltpu.VMEM(((most + BATCH) * GROUP, D), jnp.bfloat16),
        pltpu.VMEM((len(arrays), PAIR * BLOCK, D), jnp.bfloat16),
        pltpu.SemaphoreType.DMA((most,)),
        pltpu.SemaphoreType.DMA((len(arrays),)),
    ]
    if more:
        out_shape.append(jax.ShapeDtypeStruct((len(order), q.shape[0]), jnp.float32))
        scratch = [pltpu.VMEM((passages, PREFIX), jnp.bfloat16), pltpu.SemaphoreType.DMA((len(arrays),))] + scratch
    return pl.pallas_call(
        functools.partial(score_kernel, b0, order, n_src * n_rel, n_rel, D ** (-0.5), PREFIX ** (-0.5)),
        out_shape=out_shape,
        in_specs=[SMEM, ANY] + [ANY] * len(arrays) + [VMEM] * len(more),
        out_specs=[VMEM] * len(out_shape),
        scratch_shapes=scratch,
        compiler_params=pltpu.CompilerParams(vmem_limit_bytes=36 * MIB),
        cost_estimate=pl.CostEstimate(flops=2 * passages * 64 * D, bytes_accessed=passages * D * 4, transcendentals=0),
    )(lists, q, *arrays, *more)


def coarse_part(heads, arrays):
    tops = jnp.concatenate([a[:, :PREFIX] for a in arrays], axis=0)
    s = jnp.einsum("qd,pd->qp", heads, tops, preferred_element_type=jnp.float32) * PREFIX ** (-0.5)
    return jnp.max(s.reshape(heads.shape[0], -1, BLOCK), axis=2).T


def pick_kernel(n_rel, slot, answers, out):
    for e in range(slot.shape[0]):
        g, s = e // SHORT, e % SHORT
        out[g * GROUP : (g + 1) * GROUP, s * BLOCK : (s + 1) * BLOCK] = answers[slot[e]]


def body(queries, corpus, shortlist):
    n_corpus = lax.axis_size("corpus")
    n_query = lax.axis_size("query")
    n_slots = n_corpus * n_query
    blk_dev = corpus.shape[0] // BLOCK
    j = lax.axis_index("query")

    def along(a, d):
        return lax.ppermute(a, "query", [(t, (t + d) % n_query) for t in range(n_query)])

    def exchange(a):
        return lax.all_to_all(a, "corpus", split_axis=0, concat_axis=0, tiled=True)

    q = lax.all_gather(queries, "corpus", axis=0, tiled=True)

    wanted = shortlist.reshape(-1)
    holder = wanted // blk_dev
    slot = (holder // n_query) * n_query + (holder - j) % n_query
    value = (jnp.arange(wanted.shape[0], dtype=jnp.int32) // SHORT) * blk_dev + wanted % blk_dev + 1
    ids = jnp.arange(n_slots, dtype=jnp.int32)
    tags = jnp.max(jnp.where(slot[None, :] == ids[:, None], value[None, :], 0), axis=1)
    tab = exchange(tags.reshape(n_corpus, n_query)).reshape(-1)
    order = [(l, r) for r in (0, 1, 3, 2) for l in range(blk_dev)]
    lists = pl.pallas_call(
        functools.partial(list_kernel, order, blk_dev, n_corpus, n_query),
        out_shape=jax.ShapeDtypeStruct((2 * n_slots + len(order) + 1,), jnp.int32),
        in_specs=[SMEM],
        out_specs=SMEM,
    )(tab)

    own = [corpus[: PAIR * BLOCK], corpus[PAIR * BLOCK :]]
    before = [along(a, 1) for a in own]
    after = [along(a, -1) for a in own]
    low, high, lists = lax.optimization_barrier((before[0], after[1], lists))
    across = [along(low, 1), along(high, -1)]

    early = own + after + before
    n_early = PAIR * len(early)
    (answers,) = score(0, order[:n_early], early, lists, q, [], n_corpus, n_query)
    heads = q[:, :PREFIX]
    c01 = coarse_part(heads, own + after)
    c3 = coarse_part(heads, before)
    c0, c1, c3 = c01[:blk_dev], along(c01[blk_dev:], 1), along(c3, -1)
    answers, c0, c1, c3 = lax.optimization_barrier((answers, c0, c1, c3))
    answers, c2 = score(n_early, order[n_early:], across, lists, q, [answers, heads], n_corpus, n_query)
    returned = exchange(answers.reshape(n_corpus, n_query * GROUP, BLOCK))

    back = jnp.stack([c0, c1, along(c2, 2), c3])
    back = back.reshape(n_query, blk_dev, n_corpus, BLOCK)
    coarse = jnp.stack(
        [lax.dynamic_index_in_dim(back, (j - t) % n_query, 0, keepdims=False) for t in range(n_query)], axis=2
    ).reshape(blk_dev, -1)

    rescored = pl.pallas_call(
        functools.partial(pick_kernel, n_query),
        out_shape=jax.ShapeDtypeStruct((queries.shape[0], SHORT * BLOCK), jnp.bfloat16),
        in_specs=[SMEM, VMEM],
        out_specs=VMEM,
    )(slot, returned.reshape(-1, GROUP, BLOCK))
    return (coarse, rescored)


def solution(mesh):
    spec = P(("corpus", "query"), None)
    return jax.shard_map(
        body, mesh=mesh, in_specs=(spec, spec, spec), out_specs=(spec, spec), check_vma=False
    )
```

```python
import functools

import jax
import jax.numpy as jnp
from jax import lax
from jax.experimental import pallas as pl
from jax.experimental.pallas import tpu as pltpu
from jax.sharding import PartitionSpec as P

D = 4096
PREFIX = 256
BLOCK = 128
GROUP = 16
SHORT = 8
BATCH = 16
PAIR = 2
TILE = 512
CUTS = 4
MIB = 2**20

SMEM = pl.BlockSpec(memory_space=pltpu.SMEM)
VMEM = pl.BlockSpec(memory_space=pltpu.VMEM)
ANY = pl.BlockSpec(memory_space=pl.ANY)


def list_kernel(order, blk_dev, n_src, n_rel, tab, slot, lists):
    most = n_src * n_rel

    def clear(n, _):
        lists[n] = 0
        return 0

    lax.fori_loop(0, 2 * most, clear, 0)
    count = jnp.int32(0)
    for b, (local, r) in enumerate(order):
        lists[2 * most + b] = count

        def scan(i, n, local=local, r=r):
            v = tab[i * n_rel + r] - 1
            hit = (v >= 0) & (v % blk_dev == local)

            @pl.when(hit)
            def _():
                lists[n] = i * BLOCK + (v // blk_dev) * GROUP
                lists[most + n] = i

            return n + hit.astype(jnp.int32)

        count = lax.fori_loop(0, n_src, scan, count)
    last = 2 * most + len(order)
    lists[last] = count

    def keep(n, _):
        lists[last + 1 + n] = slot[n]
        return 0

    lax.fori_loop(0, slot.shape[0], keep, 0)


def score_kernel(b0, order, most, n_rel, scale, head_scale, lists, q_ref, *refs):
    n_arrays = len(order) // PAIR
    arrays, refs = refs[:n_arrays], refs[n_arrays:]
    coarse = len(refs) > 5
    if coarse:
        _, heads, out, best, found, fsem, cbuf, hsems, qbuf, abuf, sems, asems = refs
    else:
        out, qbuf, abuf, sems, asems = refs
    wide = PAIR * BLOCK
    wholes = [pltpu.make_async_copy(ref, abuf.at[k], asems.at[k]) for k, ref in enumerate(arrays)]
    if coarse:
        tops = [
            pltpu.make_async_copy(ref.at[:, pl.ds(0, PREFIX)], cbuf.at[pl.ds(k * wide, wide)], hsems.at[k])
            for k, ref in enumerate(arrays)
        ]
        for copy in tops:
            copy.start()

    def row_copy(src_row, pos):
        return pltpu.make_async_copy(
            q_ref.at[pl.ds(pl.multiple_of(src_row, GROUP), GROUP)],
            qbuf.at[pl.ds(pl.multiple_of(pos * GROUP, GROUP), GROUP)],
            sems.at[pos],
        )

    first = 2 * most + b0
    base = lists[first]
    total = lists[first + len(order)] - base

    def start(n, _):
        row_copy(lists[base + n], n).start()
        return 0

    lax.fori_loop(0, total, start, 0)
    for copy in wholes:
        copy.start()
    if coarse:
        for copy in tops:
            copy.wait()

        def tile(t, _):
            span = pl.ds(pl.multiple_of(t * TILE, TILE), TILE)
            h = heads[span, :]
            for k in range(n_arrays):
                s = lax.dot_general(
                    cbuf[k * wide : (k + 1) * wide], h, (((1,), (1,)), ((), ())), preferred_element_type=jnp.float32
                )
                top = jnp.max(s.reshape(PAIR, BLOCK, TILE), axis=1) * head_scale
                best[k * PAIR : (k + 1) * PAIR, span] = top
            return 0

        lax.fori_loop(0, heads.shape[0] // TILE, tile, 0, unroll=2)

    waited = jnp.int32(0)
    for k in range(n_arrays):
        wholes[k].wait()
        lo, mid, hi = [lists[first + PAIR * k + n] - base for n in range(PAIR + 1)]
        rel = order[PAIR * k][1]

        def step(t, waited, lo=lo, mid=mid, hi=hi, pair=abuf.at[k], rel=rel):
            at = lo + t * BATCH
            upto = jnp.minimum(at + BATCH, total)

            def wait(n, _):
                row_copy(0, n).wait()
                return 0

            lax.fori_loop(waited, upto, wait, 0)
            part = qbuf[pl.ds(pl.multiple_of(at * GROUP, GROUP), BATCH * GROUP), :]
            s = lax.dot_general(pair[...], part, (((1,), (1,)), ((), ())), preferred_element_type=jnp.float32)
            s = s.T * scale
            for m in range(BATCH):

                @pl.when(at + m < hi)
                def _():
                    both = s[m * GROUP : (m + 1) * GROUP]
                    one = jnp.where(at + m < mid, both[:, :BLOCK], both[:, BLOCK:]).astype(out.dtype)
                    source = lists[most + base + at + m]
                    if coarse:
                        found[source] = one
                    else:
                        out[source, rel] = one

            return jnp.maximum(waited, upto)

        waited = lax.fori_loop(0, (hi - lo + BATCH - 1) // BATCH, step, waited)

    if coarse:
        put = pltpu.make_async_copy(found, out.at[:, order[0][1]], fsem)
        put.start()
        put.wait()


def score(b0, order, arrays, lists, q, more, n_src, n_rel):
    most = n_src * len({r for _, r in order})
    passages = len(order) * BLOCK
    out_shape = [jax.ShapeDtypeStruct((n_src, n_rel, GROUP, BLOCK), jnp.bfloat16)]
    scratch = [
        pltpu.VMEM(((most + BATCH) * GROUP, D), jnp.bfloat16),
        pltpu.VMEM((len(arrays), PAIR * BLOCK, D), jnp.bfloat16),
        pltpu.SemaphoreType.DMA((most,)),
        pltpu.SemaphoreType.DMA((len(arrays),)),
    ]
    if more:
        out_shape.append(jax.ShapeDtypeStruct((len(order), q.shape[0]), jnp.float32))
        scratch = [
            pltpu.VMEM((n_src, GROUP, BLOCK), jnp.bfloat16),
            pltpu.SemaphoreType.DMA(()),
            pltpu.VMEM((passages, PREFIX), jnp.bfloat16),
            pltpu.SemaphoreType.DMA((len(arrays),)),
        ] + scratch
    return pl.pallas_call(
        functools.partial(score_kernel, b0, order, n_src * n_rel, n_rel, D ** (-0.5), PREFIX ** (-0.5)),
        out_shape=out_shape,
        in_specs=[SMEM, ANY] + [ANY] * len(arrays) + [ANY, VMEM][: len(more)],
        out_specs=[ANY, VMEM] if more else [VMEM],
        input_output_aliases={2 + len(arrays): 0} if more else {},
        scratch_shapes=scratch,
        compiler_params=pltpu.CompilerParams(vmem_limit_bytes=36 * MIB),
        cost_estimate=pl.CostEstimate(flops=2 * passages * 64 * D, bytes_accessed=passages * D * 4, transcendentals=0),
    )(lists, q, *arrays, *more)


def cut_kernel(row, source, out, sems):
    rows = out.shape[0] // CUTS
    copies = [
        pltpu.make_async_copy(source.at[pl.ds(row + k * rows, rows)], out.at[pl.ds(k * rows, rows)], sems.at[k])
        for k in range(CUTS)
    ]
    for copy in copies:
        copy.start()
    for copy in copies:
        copy.wait()


def cut(source, row, rows):
    return pl.pallas_call(
        functools.partial(cut_kernel, row),
        out_shape=jax.ShapeDtypeStruct((rows, source.shape[1]), source.dtype),
        in_specs=[ANY],
        out_specs=VMEM,
        scratch_shapes=[pltpu.SemaphoreType.DMA((CUTS,))],
        compiler_params=pltpu.CompilerParams(vmem_limit_bytes=8 * MIB),
    )(source)


def coarse_part(heads, arrays):
    tops = jnp.concatenate([a[:, :PREFIX] for a in arrays], axis=0)
    s = jnp.einsum("qd,pd->qp", heads, tops, preferred_element_type=jnp.float32) * PREFIX ** (-0.5)
    return jnp.max(s.reshape(heads.shape[0], -1, BLOCK), axis=2).T


def pick_kernel(n_entries, lists, answers, out):
    at = lists.shape[0] - n_entries
    for e in range(n_entries):
        g, s = e // SHORT, e % SHORT
        out[g * GROUP : (g + 1) * GROUP, s * BLOCK : (s + 1) * BLOCK] = answers[lists[at + e]]


def body(queries, corpus, shortlist):
    n_corpus = lax.axis_size("corpus")
    n_query = lax.axis_size("query")
    n_slots = n_corpus * n_query
    blk_dev = corpus.shape[0] // BLOCK
    j = lax.axis_index("query")

    def along(a, d):
        return lax.ppermute(a, "query", [(t, (t + d) % n_query) for t in range(n_query)])

    def exchange(a):
        return lax.all_to_all(a, "corpus", split_axis=0, concat_axis=0, tiled=True)

    q = lax.all_gather(queries, "corpus", axis=0, tiled=True)

    wanted = shortlist.reshape(-1)
    holder = wanted // blk_dev
    slot = (holder // n_query) * n_query + (holder - j) % n_query
    value = (jnp.arange(wanted.shape[0], dtype=jnp.int32) // SHORT) * blk_dev + wanted % blk_dev + 1
    ids = jnp.arange(n_slots, dtype=jnp.int32)
    tags = jnp.max(jnp.where(slot[None, :] == ids[:, None], value[None, :], 0), axis=1)
    tab = exchange(tags.reshape(n_corpus, n_query)).reshape(-1)
    order = [(l, r) for r in (0, 1, 3, 2) for l in range(blk_dev)]
    lists = pl.pallas_call(
        functools.partial(list_kernel, order, blk_dev, n_corpus, n_query),
        out_shape=jax.ShapeDtypeStruct((2 * n_slots + len(order) + 1 + slot.shape[0],), jnp.int32),
        in_specs=[SMEM, SMEM],
        out_specs=SMEM,
    )(tab, slot)

    own = [cut(corpus, 0, PAIR * BLOCK), cut(corpus, PAIR * BLOCK, PAIR * BLOCK)]
    before = [along(a, 1) for a in own]
    after = [along(a, -1) for a in own]
    low, high, lists = lax.optimization_barrier((before[0], after[1], lists))
    across = [along(low, 1), along(high, -1)]

    early = own + after + before
    n_early = PAIR * len(early)
    (answers,) = score(0, order[:n_early], early, lists, q, [], n_corpus, n_query)
    heads = q[:, :PREFIX]
    c01 = coarse_part(heads, own + after)
    c3 = coarse_part(heads, before)
    answers, c01, c3 = lax.optimization_barrier((answers, c01, c3))
    answers, c2 = score(n_early, order[n_early:], across, lists, q, [answers, heads], n_corpus, n_query)
    c01, c2, c3 = lax.optimization_barrier((c01, c2, c3))
    c0, c1 = c01[:blk_dev], c01[blk_dev:]
    returned = exchange(answers.reshape(n_corpus, n_query * GROUP, BLOCK))

    back = jnp.stack([c0, along(c1, 1), along(c2, 2), along(c3, -1)])
    back = back.reshape(n_query, blk_dev, n_corpus, BLOCK)
    coarse = jnp.stack(
        [lax.dynamic_index_in_dim(back, (j - t) % n_query, 0, keepdims=False) for t in range(n_query)], axis=2
    ).reshape(blk_dev, -1)

    rescored = pl.pallas_call(
        functools.partial(pick_kernel, wanted.shape[0]),
        out_shape=jax.ShapeDtypeStruct((queries.shape[0], SHORT * BLOCK), jnp.bfloat16),
        in_specs=[SMEM, VMEM],
        out_specs=VMEM,
    )(lists, returned.reshape(-1, GROUP, BLOCK))
    return (coarse, rescored)


def solution(mesh):
    spec = P(("corpus", "query"), None)
    return jax.shard_map(
        body, mesh=mesh, in_specs=(spec, spec, spec), out_specs=(spec, spec), check_vma=False
    )
```

```python
import functools

import jax
import jax.numpy as jnp
from jax import lax
from jax.experimental import pallas as pl
from jax.experimental.pallas import tpu as pltpu
from jax.sharding import PartitionSpec as P

D = 4096
PREFIX = 256
BLOCK = 128
GROUP = 16
SHORT = 8
BATCH = 16
PAIR = 2
TILE = 512
CUTS = 4
MIB = 2**20

SMEM = pl.BlockSpec(memory_space=pltpu.SMEM)
VMEM = pl.BlockSpec(memory_space=pltpu.VMEM)
ANY = pl.BlockSpec(memory_space=pl.ANY)


def list_kernel(order, blk_dev, n_src, n_rel, tab, slot, lists):
    most = n_src * n_rel

    def clear(n, _):
        lists[n] = 0
        return 0

    lax.fori_loop(0, 2 * most, clear, 0)
    count = jnp.int32(0)
    for b, (local, r) in enumerate(order):
        lists[2 * most + b] = count

        def scan(i, n, local=local, r=r):
            v = tab[i * n_rel + r] - 1
            hit = (v >= 0) & (v % blk_dev == local)

            @pl.when(hit)
            def _():
                lists[n] = i * BLOCK + (v // blk_dev) * GROUP
                lists[most + n] = i

            return n + hit.astype(jnp.int32)

        count = lax.fori_loop(0, n_src, scan, count)
    last = 2 * most + len(order)
    lists[last] = count

    def keep(n, _):
        lists[last + 1 + n] = slot[n]
        return 0

    lax.fori_loop(0, slot.shape[0], keep, 0)


def score_kernel(b0, order, most, n_rel, scale, head_scale, lists, q_ref, *refs):
    n_arrays = len(order) // PAIR
    arrays, refs = refs[:n_arrays], refs[n_arrays:]
    coarse = len(refs) > 5
    if coarse:
        _, heads, out, best, found, fsem, cbuf, hsems, qbuf, abuf, sems, asems = refs
    else:
        out, qbuf, abuf, sems, asems = refs
    wide = PAIR * BLOCK
    wholes = [pltpu.make_async_copy(ref, abuf.at[k], asems.at[k]) for k, ref in enumerate(arrays)]
    if coarse:
        tops = [
            pltpu.make_async_copy(ref.at[:, pl.ds(0, PREFIX)], cbuf.at[pl.ds(k * wide, wide)], hsems.at[k])
            for k, ref in enumerate(arrays)
        ]
        for copy in tops:
            copy.start()

    def row_copy(src_row, pos):
        return pltpu.make_async_copy(
            q_ref.at[pl.ds(pl.multiple_of(src_row, GROUP), GROUP)],
            qbuf.at[pl.ds(pl.multiple_of(pos * GROUP, GROUP), GROUP)],
            sems.at[pos],
        )

    first = 2 * most + b0
    base = lists[first]
    total = lists[first + len(order)] - base

    def start(n, _):
        row_copy(lists[base + n], n).start()
        return 0

    lax.fori_loop(0, total, start, 0)
    for copy in wholes:
        copy.start()
    if coarse:
        for copy in tops:
            copy.wait()

        def tile(t, _):
            span = pl.ds(pl.multiple_of(t * TILE, TILE), TILE)
            h = heads[span, :]
            for k in range(n_arrays):
                s = lax.dot_general(
                    cbuf[k * wide : (k + 1) * wide], h, (((1,), (1,)), ((), ())), preferred_element_type=jnp.float32
                )
                top = jnp.max(s.reshape(PAIR, BLOCK, TILE), axis=1) * head_scale
                best[k * PAIR : (k + 1) * PAIR, span] = top
            return 0

        lax.fori_loop(0, heads.shape[0] // TILE, tile, 0, unroll=2)

    waited = jnp.int32(0)
    for k in range(n_arrays):
        wholes[k].wait()
        lo, mid, hi = [lists[first + PAIR * k + n] - base for n in range(PAIR + 1)]
        rel = order[PAIR * k][1]

        def step(t, waited, lo=lo, mid=mid, hi=hi, pair=abuf.at[k], rel=rel):
            at = lo + t * BATCH
            upto = jnp.minimum(at + BATCH, total)

            def wait(n, _):
                row_copy(0, n).wait()
                return 0

            lax.fori_loop(waited, upto, wait, 0)
            part = qbuf[pl.ds(pl.multiple_of(at * GROUP, GROUP), BATCH * GROUP), :]
            s = lax.dot_general(pair[...], part, (((1,), (1,)), ((), ())), preferred_element_type=jnp.float32)
            s = s.T * scale
            for m in range(BATCH):

                @pl.when(at + m < hi)
                def _():
                    both = s[m * GROUP : (m + 1) * GROUP]
                    one = jnp.where(at + m < mid, both[:, :BLOCK], both[:, BLOCK:]).astype(out.dtype)
                    source = lists[most + base + at + m]
                    if coarse:
                        found[source] = one
                    else:
                        out[source, rel] = one

            return jnp.maximum(waited, upto)

        waited = lax.fori_loop(0, (hi - lo + BATCH - 1) // BATCH, step, waited)

    if coarse:
        put = pltpu.make_async_copy(found, out.at[:, order[0][1]], fsem)
        put.start()
        put.wait()


def score(b0, order, arrays, lists, q, more, n_src, n_rel):
    most = n_src * len({r for _, r in order})
    passages = len(order) * BLOCK
    out_shape = [jax.ShapeDtypeStruct((n_src, n_rel, GROUP, BLOCK), jnp.bfloat16)]
    scratch = [
        pltpu.VMEM(((most + BATCH) * GROUP, D), jnp.bfloat16),
        pltpu.VMEM((len(arrays), PAIR * BLOCK, D), jnp.bfloat16),
        pltpu.SemaphoreType.DMA((most,)),
        pltpu.SemaphoreType.DMA((len(arrays),)),
    ]
    if more:
        out_shape.append(jax.ShapeDtypeStruct((len(order), q.shape[0]), jnp.float32))
        scratch = [
            pltpu.VMEM((n_src, GROUP, BLOCK), jnp.bfloat16),
            pltpu.SemaphoreType.DMA(()),
            pltpu.VMEM((passages, PREFIX), jnp.bfloat16),
            pltpu.SemaphoreType.DMA((len(arrays),)),
        ] + scratch
    return pl.pallas_call(
        functools.partial(score_kernel, b0, order, n_src * n_rel, n_rel, D ** (-0.5), PREFIX ** (-0.5)),
        out_shape=out_shape,
        in_specs=[SMEM, ANY] + [ANY] * len(arrays) + [ANY, VMEM][: len(more)],
        out_specs=[ANY, VMEM] if more else [VMEM],
        input_output_aliases={2 + len(arrays): 0} if more else {},
        scratch_shapes=scratch,
        compiler_params=pltpu.CompilerParams(vmem_limit_bytes=36 * MIB),
        cost_estimate=pl.CostEstimate(flops=2 * passages * 64 * D, bytes_accessed=passages * D * 4, transcendentals=0),
    )(lists, q, *arrays, *more)


def cut_kernel(source, *refs):
    outs, sems = refs[:PAIR], refs[PAIR]
    rows = outs[0].shape[0] // CUTS
    copies = [
        pltpu.make_async_copy(
            source.at[pl.ds((n * CUTS + k) * rows, rows)], out.at[pl.ds(k * rows, rows)], sems.at[n * CUTS + k]
        )
        for n, out in enumerate(outs)
        for k in range(CUTS)
    ]
    for copy in copies:
        copy.start()
    for copy in copies:
        copy.wait()


def cut(source):
    half = jax.ShapeDtypeStruct((source.shape[0] // PAIR, source.shape[1]), source.dtype)
    return pl.pallas_call(
        cut_kernel,
        out_shape=[half] * PAIR,
        in_specs=[ANY],
        out_specs=[VMEM] * PAIR,
        scratch_shapes=[pltpu.SemaphoreType.DMA((PAIR * CUTS,))],
        compiler_params=pltpu.CompilerParams(vmem_limit_bytes=55 * MIB),
    )(source)


def coarse_part(heads, arrays):
    tops = jnp.concatenate([a[:, :PREFIX] for a in arrays], axis=0)
    s = jnp.einsum("qd,pd->qp", heads, tops, preferred_element_type=jnp.float32) * PREFIX ** (-0.5)
    return jnp.max(s.reshape(heads.shape[0], -1, BLOCK), axis=2).T


def pick_kernel(n_entries, lists, answers, out):
    at = lists.shape[0] - n_entries
    for e in range(n_entries):
        g, s = e // SHORT, e % SHORT
        out[g * GROUP : (g + 1) * GROUP, s * BLOCK : (s + 1) * BLOCK] = answers[lists[at + e]]


def body(queries, corpus, shortlist):
    n_corpus = lax.axis_size("corpus")
    n_query = lax.axis_size("query")
    n_slots = n_corpus * n_query
    blk_dev = corpus.shape[0] // BLOCK
    j = lax.axis_index("query")

    def along(a, d):
        return lax.ppermute(a, "query", [(t, (t + d) % n_query) for t in range(n_query)])

    def exchange(a):
        return lax.all_to_all(a, "corpus", split_axis=0, concat_axis=0, tiled=True)

    q = lax.all_gather(queries, "corpus", axis=0, tiled=True)

    wanted = shortlist.reshape(-1)
    holder = wanted // blk_dev
    slot = (holder // n_query) * n_query + (holder - j) % n_query
    value = (jnp.arange(wanted.shape[0], dtype=jnp.int32) // SHORT) * blk_dev + wanted % blk_dev + 1
    ids = jnp.arange(n_slots, dtype=jnp.int32)
    tags = jnp.max(jnp.where(slot[None, :] == ids[:, None], value[None, :], 0), axis=1)
    tab = exchange(tags.reshape(n_corpus, n_query)).reshape(-1)
    order = [(l, r) for r in (0, 1, 3, 2) for l in range(blk_dev)]
    lists = pl.pallas_call(
        functools.partial(list_kernel, order, blk_dev, n_corpus, n_query),
        out_shape=jax.ShapeDtypeStruct((2 * n_slots + len(order) + 1 + slot.shape[0],), jnp.int32),
        in_specs=[SMEM, SMEM],
        out_specs=SMEM,
    )(tab, slot)

    own = list(cut(corpus))
    before = [along(a, 1) for a in own]
    after = [along(a, -1) for a in own]
    low, high, lists = lax.optimization_barrier((before[0], after[1], lists))
    across = [along(low, 1), along(high, -1)]

    early = own + after + before
    n_early = PAIR * len(early)
    (answers,) = score(0, order[:n_early], early, lists, q, [], n_corpus, n_query)
    heads = q[:, :PREFIX]
    c01 = coarse_part(heads, own + after)
    c3 = coarse_part(heads, before)
    answers, c01, c3 = lax.optimization_barrier((answers, c01, c3))
    answers, c2 = score(n_early, order[n_early:], across, lists, q, [answers, heads], n_corpus, n_query)
    c01, c2, c3 = lax.optimization_barrier((c01, c2, c3))
    c0, c1 = c01[:blk_dev], c01[blk_dev:]
    returned = exchange(answers.reshape(n_corpus, n_query * GROUP, BLOCK))

    back = jnp.stack([c0, along(c1, 1), along(c2, 2), along(c3, -1)])
    back = back.reshape(n_query, blk_dev, n_corpus, BLOCK)
    coarse = jnp.stack(
        [lax.dynamic_index_in_dim(back, (j - t) % n_query, 0, keepdims=False) for t in range(n_query)], axis=2
    ).reshape(blk_dev, -1)

    rescored = pl.pallas_call(
        functools.partial(pick_kernel, wanted.shape[0]),
        out_shape=jax.ShapeDtypeStruct((queries.shape[0], SHORT * BLOCK), jnp.bfloat16),
        in_specs=[SMEM, VMEM],
        out_specs=VMEM,
    )(lists, returned.reshape(-1, GROUP, BLOCK))
    return (coarse, rescored)


def solution(mesh):
    spec = P(("corpus", "query"), None)
    return jax.shard_map(
        body, mesh=mesh, in_specs=(spec, spec, spec), out_specs=(spec, spec), check_vma=False
    )
```

```python
import functools

import jax
import jax.numpy as jnp
from jax import lax
from jax.experimental import pallas as pl
from jax.experimental.pallas import tpu as pltpu
from jax.sharding import PartitionSpec as P

D = 4096
PREFIX = 256
BLOCK = 128
GROUP = 16
SHORT = 8
BATCH = 16
PAIR = 2
TILE = 512
CUTS = 4
MIB = 2**20

SMEM = pl.BlockSpec(memory_space=pltpu.SMEM)
VMEM = pl.BlockSpec(memory_space=pltpu.VMEM)
ANY = pl.BlockSpec(memory_space=pl.ANY)


def list_kernel(order, blk_dev, n_src, n_rel, tab, slot, lists):
    most = n_src * n_rel

    def clear(n, _):
        lists[n] = 0
        return 0

    lax.fori_loop(0, 2 * most, clear, 0)
    count = jnp.int32(0)
    for b, (local, r) in enumerate(order):
        lists[2 * most + b] = count

        def scan(i, n, local=local, r=r):
            v = tab[i * n_rel + r] - 1
            hit = (v >= 0) & (v % blk_dev == local)

            @pl.when(hit)
            def _():
                lists[n] = i * BLOCK + (v // blk_dev) * GROUP
                lists[most + n] = i

            return n + hit.astype(jnp.int32)

        count = lax.fori_loop(0, n_src, scan, count)
    last = 2 * most + len(order)
    lists[last] = count

    def keep(n, _):
        lists[last + 1 + n] = slot[n]
        return 0

    lax.fori_loop(0, slot.shape[0], keep, 0)


def score_kernel(b0, order, most, n_rel, scale, head_scale, lists, q_ref, *refs):
    n_arrays = len(order) // PAIR
    arrays, refs = refs[:n_arrays], refs[n_arrays:]
    coarse = len(refs) > 5
    if coarse:
        _, heads, out, best, found, fsem, cbuf, hsems, qbuf, abuf, sems, asems = refs
    else:
        out, qbuf, abuf, sems, asems = refs
    wide = PAIR * BLOCK
    wholes = [pltpu.make_async_copy(ref, abuf.at[k], asems.at[k]) for k, ref in enumerate(arrays)]
    if coarse:
        tops = [
            pltpu.make_async_copy(ref.at[:, pl.ds(0, PREFIX)], cbuf.at[pl.ds(k * wide, wide)], hsems.at[k])
            for k, ref in enumerate(arrays)
        ]
        for copy in tops:
            copy.start()

    def row_copy(src_row, pos):
        return pltpu.make_async_copy(
            q_ref.at[pl.ds(pl.multiple_of(src_row, GROUP), GROUP)],
            qbuf.at[pl.ds(pl.multiple_of(pos * GROUP, GROUP), GROUP)],
            sems.at[pos],
        )

    first = 2 * most + b0
    base = lists[first]
    total = lists[first + len(order)] - base

    def start(n, _):
        row_copy(lists[base + n], n).start()
        return 0

    lax.fori_loop(0, total, start, 0)
    for copy in wholes:
        copy.start()
    if coarse:
        for copy in tops:
            copy.wait()

        def tile(t, _):
            span = pl.ds(pl.multiple_of(t * TILE, TILE), TILE)
            h = heads[span, :]
            for k in range(n_arrays):
                s = lax.dot_general(
                    cbuf[k * wide : (k + 1) * wide], h, (((1,), (1,)), ((), ())), preferred_element_type=jnp.float32
                )
                top = jnp.max(s.reshape(PAIR, BLOCK, TILE), axis=1) * head_scale
                best[k * PAIR : (k + 1) * PAIR, span] = top
            return 0

        lax.fori_loop(0, heads.shape[0] // TILE, tile, 0, unroll=2)

    waited = jnp.int32(0)
    for k in range(n_arrays):
        wholes[k].wait()
        lo, mid, hi = [lists[first + PAIR * k + n] - base for n in range(PAIR + 1)]
        rel = order[PAIR * k][1]

        def step(t, waited, lo=lo, mid=mid, hi=hi, pair=abuf.at[k], rel=rel):
            at = lo + t * BATCH
            upto = jnp.minimum(at + BATCH, total)

            def wait(n, _):
                row_copy(0, n).wait()
                return 0

            lax.fori_loop(waited, upto, wait, 0)
            part = qbuf[pl.ds(pl.multiple_of(at * GROUP, GROUP), BATCH * GROUP), :]
            s = lax.dot_general(pair[...], part, (((1,), (1,)), ((), ())), preferred_element_type=jnp.float32)
            s = s.T * scale
            for m in range(BATCH):

                @pl.when(at + m < hi)
                def _():
                    both = s[m * GROUP : (m + 1) * GROUP]
                    one = jnp.where(at + m < mid, both[:, :BLOCK], both[:, BLOCK:]).astype(out.dtype)
                    source = lists[most + base + at + m]
                    if coarse:
                        found[source] = one
                    else:
                        out[source, rel] = one

            return jnp.maximum(waited, upto)

        waited = lax.fori_loop(0, (hi - lo + BATCH - 1) // BATCH, step, waited)

    if coarse:
        put = pltpu.make_async_copy(found, out.at[:, order[0][1]], fsem)
        put.start()
        put.wait()


def score(b0, order, arrays, lists, q, more, n_src, n_rel):
    most = n_src * len({r for _, r in order})
    passages = len(order) * BLOCK
    out_shape = [jax.ShapeDtypeStruct((n_src, n_rel, GROUP, BLOCK), jnp.bfloat16)]
    scratch = [
        pltpu.VMEM(((most + BATCH) * GROUP, D), jnp.bfloat16),
        pltpu.VMEM((len(arrays), PAIR * BLOCK, D), jnp.bfloat16),
        pltpu.SemaphoreType.DMA((most,)),
        pltpu.SemaphoreType.DMA((len(arrays),)),
    ]
    if more:
        out_shape.append(jax.ShapeDtypeStruct((len(order), q.shape[0]), jnp.float32))
        scratch = [
            pltpu.VMEM((n_src, GROUP, BLOCK), jnp.bfloat16),
            pltpu.SemaphoreType.DMA(()),
            pltpu.VMEM((passages, PREFIX), jnp.bfloat16),
            pltpu.SemaphoreType.DMA((len(arrays),)),
        ] + scratch
    return pl.pallas_call(
        functools.partial(score_kernel, b0, order, n_src * n_rel, n_rel, D ** (-0.5), PREFIX ** (-0.5)),
        out_shape=out_shape,
        in_specs=[SMEM, ANY] + [ANY] * len(arrays) + [ANY, VMEM][: len(more)],
        out_specs=[ANY, VMEM] if more else [VMEM],
        input_output_aliases={2 + len(arrays): 0} if more else {},
        scratch_shapes=scratch,
        compiler_params=pltpu.CompilerParams(vmem_limit_bytes=36 * MIB),
        cost_estimate=pl.CostEstimate(flops=2 * passages * 64 * D, bytes_accessed=passages * D * 4, transcendentals=0),
    )(lists, q, *arrays, *more)


def cut_kernel(source, *refs):
    outs, sems = refs[:PAIR], refs[PAIR]
    rows = outs[0].shape[0] // CUTS
    copies = [
        pltpu.make_async_copy(
            source.at[pl.ds((n * CUTS + k) * rows, rows)], out.at[pl.ds(k * rows, rows)], sems.at[n * CUTS + k]
        )
        for n, out in enumerate(outs)
        for k in range(CUTS)
    ]
    for copy in copies:
        copy.start()
    for copy in copies:
        copy.wait()


def cut(source):
    half = jax.ShapeDtypeStruct((source.shape[0] // PAIR, source.shape[1]), source.dtype)
    return pl.pallas_call(
        cut_kernel,
        out_shape=[half] * PAIR,
        in_specs=[ANY],
        out_specs=[VMEM] * PAIR,
        scratch_shapes=[pltpu.SemaphoreType.DMA((PAIR * CUTS,))],
        compiler_params=pltpu.CompilerParams(vmem_limit_bytes=55 * MIB),
    )(source)


def coarse_part(heads, arrays):
    tops = jnp.concatenate([a[:, :PREFIX] for a in arrays], axis=0)
    s = jnp.einsum("qd,pd->qp", heads, tops, preferred_element_type=jnp.float32) * PREFIX ** (-0.5)
    return jnp.max(s.reshape(heads.shape[0], -1, BLOCK), axis=2).T


def pick_kernel(n_entries, lists, answers, out):
    at = lists.shape[0] - n_entries
    for e in range(n_entries):
        g, s = e // SHORT, e % SHORT
        out[g * GROUP : (g + 1) * GROUP, s * BLOCK : (s + 1) * BLOCK] = answers[lists[at + e]]


def body(queries, corpus, shortlist):
    n_corpus = lax.axis_size("corpus")
    n_query = lax.axis_size("query")
    n_slots = n_corpus * n_query
    blk_dev = corpus.shape[0] // BLOCK
    j = lax.axis_index("query")

    def along(a, d):
        return lax.ppermute(a, "query", [(t, (t + d) % n_query) for t in range(n_query)])

    def exchange(a):
        return lax.all_to_all(a, "corpus", split_axis=0, concat_axis=0, tiled=True)

    q = lax.all_gather(queries, "corpus", axis=0, tiled=True)

    wanted = shortlist.reshape(-1)
    holder = wanted // blk_dev
    slot = (holder // n_query) * n_query + (holder - j) % n_query
    value = (jnp.arange(wanted.shape[0], dtype=jnp.int32) // SHORT) * blk_dev + wanted % blk_dev + 1
    ids = jnp.arange(n_slots, dtype=jnp.int32)
    tags = jnp.max(jnp.where(slot[None, :] == ids[:, None], value[None, :], 0), axis=1)
    tab = exchange(tags.reshape(n_corpus, n_query)).reshape(-1)
    order = [(l, r) for r in (0, 1, 3, 2) for l in range(blk_dev)]
    lists = pl.pallas_call(
        functools.partial(list_kernel, order, blk_dev, n_corpus, n_query),
        out_shape=jax.ShapeDtypeStruct((2 * n_slots + len(order) + 1 + slot.shape[0],), jnp.int32),
        in_specs=[SMEM, SMEM],
        out_specs=SMEM,
    )(tab, slot)

    own = list(cut(corpus))
    before = [along(a, 1) for a in own]
    after = [along(a, -1) for a in own]
    low, high, lists = lax.optimization_barrier((before[0], after[1], lists))
    across = [along(low, 1), along(high, -1)]

    early = own + after + before
    n_early = PAIR * len(early)
    (answers,) = score(0, order[:n_early], early, lists, q, [], n_corpus, n_query)
    answers, heads = lax.optimization_barrier((answers, q[:, :PREFIX]))
    c01 = coarse_part(heads, own + after)
    c3 = coarse_part(heads, before)
    answers, c01, c3 = lax.optimization_barrier((answers, c01, c3))
    answers, c2 = score(n_early, order[n_early:], across, lists, q, [answers, heads], n_corpus, n_query)
    c01, c2, c3 = lax.optimization_barrier((c01, c2, c3))
    c0, c1 = c01[:blk_dev], c01[blk_dev:]
    returned = exchange(answers.reshape(n_corpus, n_query * GROUP, BLOCK))

    back = jnp.stack([c0, along(c1, 1), along(c2, 2), along(c3, -1)])
    back = back.reshape(n_query, blk_dev, n_corpus, BLOCK)
    coarse = jnp.stack(
        [lax.dynamic_index_in_dim(back, (j - t) % n_query, 0, keepdims=False) for t in range(n_query)], axis=2
    ).reshape(blk_dev, -1)

    rescored = pl.pallas_call(
        functools.partial(pick_kernel, wanted.shape[0]),
        out_shape=jax.ShapeDtypeStruct((queries.shape[0], SHORT * BLOCK), jnp.bfloat16),
        in_specs=[SMEM, VMEM],
        out_specs=VMEM,
    )(lists, returned.reshape(-1, GROUP, BLOCK))
    return (coarse, rescored)


def solution(mesh):
    spec = P(("corpus", "query"), None)
    return jax.shard_map(
        body, mesh=mesh, in_specs=(spec, spec, spec), out_specs=(spec, spec), check_vma=False
    )
```
